32 devices in a mesh: dom: 32 (over z, y, x, core).
Axes of the slice: x: 2, y: 2, z: 4, core: 2. Of those that a mesh axis runs over, the one named last changes fastest.
Arguments:
- blocks: bfloat16 [4096, 128, 128], P('dom'), may hold values from 2.4e-05 to 0.161
- col_index: int32 [32, 128], P('dom'), may hold values from 0 to 79, as said below
- row_offsets: int32 [32, 33], P('dom'), may hold values from 0 to 128, as said below
- send_index: int32 [32, 6, 8], P('dom'), may hold values from 0 to 31, as said below
- deg_scale: float32 [131072], P('dom'), may hold values from 0.5 to 1
- seeds: float32 [16, 131072], P(None, 'dom'), may hold values from 0.25 to 2
Outputs:
- spread: float32 [16, 131072], P(None, 'dom')
The draws below stay inside these ranges and needn't reach their ends.
Inputs may be any that keep to these rules, and one draw needn't show every extreme that they name: In every partition the offsets start at 0 and rise by 1 to 4 per block row; slots from row_offsets[p, 32] on are unused; some partition uses all 128 slots. `col_index`: the first slot of block row r names the partition's own block r; entries below 32 name own blocks, the others received blocks. `send_index`: each list names 8 distinct blocks of the sending partition; its six lists together name every one of its blocks.
All inputs are finite; a program needn't handle non-finite values.
Results may differ from the reference program's by a relative error of at most 0.0003.
Values may be sent and summed in bfloat16 or wider, within the bound.
A program may use at most 64 MiB of HBM per device.

```python
import math
import jax
import jax.numpy as jnp
from jax import lax

C = 16
BLK = 128
RB = 32
MAXR = 4
ITERS = 4
HB = 8
NNZ = 128
EXT = 80
DOMAINS = 32
ROWS = 131072
NNZ_ALL = 4096


def row_layout(key):
    first_key, second_key = jax.random.split(jax.random.fold_in(key, 11))
    counts = jax.random.randint(first_key, (DOMAINS, RB), 1, MAXR + 1)
    fullest = jax.random.randint(second_key, (), 0, DOMAINS)
    counts = jnp.where((jnp.arange(DOMAINS) == fullest)[:, None], MAXR, counts)
    offsets = jnp.concatenate([jnp.zeros((DOMAINS, 1), jnp.int32), jnp.cumsum(counts, axis=1).astype(jnp.int32)], axis=1)
    return (offsets, fullest)


def draw_row_offsets(key, part):
    offsets, fullest = row_layout(key)
    return offsets.astype(jnp.int32)


def draw_col_index(key, part):
    offsets, fullest = row_layout(key)
    slots = jnp.arange(NNZ, dtype=jnp.int32)
    starts = offsets[:, :RB]
    is_first = (starts[:, :, None] == slots[None, None, :]).astype(jnp.int32)
    own_row = jnp.sum(is_first * jnp.arange(RB, dtype=jnp.int32)[None, :, None], axis=1)
    has_first = jnp.sum(is_first, axis=1) > 0
    others = jax.random.randint(jax.random.fold_in(key, 23), (DOMAINS, NNZ), 0, EXT)
    columns = jnp.where(has_first, own_row, others)
    last = (jnp.arange(DOMAINS) == fullest)[:, None] & (slots == NNZ - 1)[None, :]
    columns = jnp.where(last, EXT - 1, columns)
    return columns.astype(jnp.int32)


def draw_send_index(key, part):
    keys = jax.random.split(jax.random.fold_in(key, 7), DOMAINS)
    perms = jax.vmap(lambda single: jax.random.permutation(single, RB))(keys)
    position = (jnp.arange(6)[:, None] * HB + jnp.arange(HB)[None, :]) % RB
    return perms[:, position].astype(jnp.int32)


def draw_blocks(key, part):
    offsets, fullest = row_layout(key)
    slots = jnp.arange(NNZ, dtype=jnp.int32)
    row_of = jnp.sum((offsets[:, 1:, None] <= slots[None, None, :]).astype(jnp.int32), axis=1)
    row_of = jnp.minimum(row_of, RB - 1).astype(jnp.int32)
    factor_key = jax.random.fold_in(key, 31)
    entry_key = jax.random.fold_in(key, 37)
    share = 1.0 / 16.0

    def one_domain(items):
        index, rows = items
        row_draw = jax.random.uniform(jax.random.fold_in(factor_key, index), (RB, BLK), jnp.float32)
        row_factor = 0.25 * jnp.exp(row_draw * math.log(4.0))
        per_slot = row_factor[rows]
        level = jax.random.uniform(jax.random.fold_in(entry_key, index), (NNZ, BLK, BLK), jnp.float32)
        near = level < share
        upper = jnp.clip(level / share, 0.0, 1.0)
        lower = jnp.clip((level - share) / (1.0 - share), 0.0, 1.0)
        strong = 0.04 * jnp.exp(upper * math.log(4.0))
        faint = 0.0001 * jnp.exp(lower * math.log(10.0))
        value = jnp.where(near, strong, faint) * per_slot[:, :, None]
        return value.astype(jnp.bfloat16)
    mapped = lax.map(one_domain, (jnp.arange(DOMAINS, dtype=jnp.int32), row_of))
    return mapped.reshape(NNZ_ALL, BLK, BLK)


def draw_seeds(key, part):
    level = jax.random.uniform(jax.random.fold_in(key, 43), (C, ROWS), jnp.float32)
    values = 0.25 * jnp.exp(level * math.log(8.0))
    return values.astype(jnp.float32)


def steps_of(stream_key, shape, cuts, low, largest):
    level, own = 1.0, jax.random.fold_in(stream_key, 6)
    for axis_at, shards_of in cuts:
        heights = jnp.exp(jax.random.uniform(jax.random.fold_in(own, axis_at), (shards_of,), jnp.float32, low / len(cuts), largest / len(cuts)))
        level = level * jnp.repeat(heights, shape[axis_at] // shards_of).reshape([-1 if axis == axis_at else 1 for axis in range(len(shape))])
    return level


def setup_inputs(seed: int = 0) -> dict:
    key_of = jax.random.split(jax.random.key(seed), 7)
    blocks = draw_blocks(jax.random.fold_in(key_of[6], 71), 0)
    col_index = draw_col_index(jax.random.fold_in(key_of[6], 71), 0)
    row_offsets = draw_row_offsets(jax.random.fold_in(key_of[6], 71), 0)
    send_index = draw_send_index(jax.random.fold_in(key_of[6], 71), 0)
    deg_scale = jnp.clip(jnp.exp(math.log(1.0) - 0.6931472 * jax.random.uniform(key_of[4], (ROWS,), jnp.float32) ** steps_of(key_of[4], (ROWS,), ((0, 32),), -0.2, 0.2)), 0.5, 1.0)
    seeds = draw_seeds(jax.random.fold_in(key_of[6], 71), 0)
    return dict(blocks=blocks, col_index=col_index, row_offsets=row_offsets, send_index=send_index, deg_scale=deg_scale, seeds=seeds)


OFFSETS = (1, -1, 2, -2, 4, -4)
ALPHA = 0.8


def reference(blocks, col_index, row_offsets, send_index, deg_scale, seeds):
    count = DOMAINS
    weights = blocks.reshape(count, NNZ, BLK, BLK)
    scale = deg_scale.reshape(count, RB, 1, BLK)
    base = seeds.reshape(C, count, RB, BLK).transpose(1, 2, 0, 3)
    slots = jnp.arange(NNZ)
    row_of = jnp.sum((row_offsets[:, 1:, None] <= slots[None, None, :]).astype(jnp.int32), axis=1)
    owners = jnp.arange(count)
    field = base

    def one_part(items):
        extended, weight, columns, rows = items
        picked = extended[columns].astype(jnp.float32)
        prods = jnp.einsum('kcj,kij->kci', picked, weight.astype(jnp.float32), precision=lax.Precision.HIGHEST)
        onehot = (rows[None, :] == jnp.arange(RB)[:, None]).astype(jnp.float32)
        return jnp.einsum('rk,kci->rci', onehot, prods, precision=lax.Precision.HIGHEST)

    for step in range(ITERS):
        scaled = (field * scale).astype(jnp.bfloat16)
        pieces = [scaled]
        for j in range(6):
            source = (owners - OFFSETS[j]) % count
            pieces.append(scaled[source[:, None], send_index[source, j]])
        extended = jnp.concatenate(pieces, axis=1)
        summed = lax.map(one_part, (extended, weights, col_index, row_of))
        field = ALPHA * scale * summed + (1.0 - ALPHA) * base
    return field.transpose(2, 0, 1, 3).reshape(C, count * RB * BLK)
```

```python
import functools

import jax
import jax.numpy as jnp
from jax import lax
from jax.experimental import pallas as pl
from jax.experimental.pallas import tpu as pltpu
from jax.sharding import PartitionSpec as P

ITERS = 4
MAXR = 4
OFFSETS = (1, -1, 2, -2, 4, -4)
ORDER = (4, 5, 2, 3, 0, 1)
ALPHA = 0.8
CHUNKS = 4


def dot_nt(a, b):
    return lax.dot_general(a, b, (((1,), (1,)), ((), ())), preferred_element_type=jnp.float32)


def kernel(n, col_ref, off_ref, lists_ref, scale_ref, seeds_ref, blocks_ref, out_ref,
           w_ref, own_ref, acc_ref, ext_refs, send_refs, w_sem, send_sem, recv_sem):
    nnz, blk = w_ref.shape[0], w_ref.shape[1]
    nrb, width = own_ref.shape[0], own_ref.shape[1]
    parts, per = lists_ref.shape[1], lists_ref.shape[2]
    none = nrb + parts * per
    me = lax.axis_index("dom")
    partners = [lax.rem(me + (o + n), n) for o in OFFSETS]

    barrier = pltpu.get_barrier_semaphore()
    for p in partners:
        pl.semaphore_signal(barrier, inc=1, device_id=(p,), device_id_type=pl.DeviceIdType.MESH)

    span = nnz // CHUNKS
    loads = []
    for c in range(CHUNKS):
        load = pltpu.make_async_copy(
            blocks_ref.at[pl.ds(c * span, span)], w_ref.at[pl.ds(c * span, span)], w_sem.at[c])
        load.start()
        loads.append(load)

    for r in range(nrb):
        cols = pl.ds(r * blk, blk)
        scaled = (seeds_ref[:, cols] * scale_ref[r:r + 1, :]).astype(jnp.bfloat16)
        own_ref[r] = scaled
        ext_refs[0][r] = scaled
    for ext in ext_refs:
        ext[none] = jnp.zeros((width, blk), jnp.bfloat16)

    pl.semaphore_wait(barrier, parts)

    copies = []
    for step in range(ITERS):
        ext, send = ext_refs[step], send_refs[step]
        flying = []
        for j in ORDER:
            for h in range(per):
                send[j * per + h] = own_ref[lists_ref[0, j, h]]
            copy = pltpu.make_async_remote_copy(
                src_ref=send.at[pl.ds(j * per, per)],
                dst_ref=ext.at[pl.ds(nrb + j * per, per)],
                send_sem=send_sem.at[step, j],
                recv_sem=recv_sem.at[step, j],
                device_id=(partners[j],),
                device_id_type=pl.DeviceIdType.MESH,
            )
            copy.start()
            flying.append(copy)
        copies += flying

        if step == 0:
            for load in loads:
                load.wait()

        def first(r, carry):
            acc_ref[r] = dot_nt(ext[r], w_ref[off_ref[0, r]])
            return carry

        lax.fori_loop(0, nrb, first, 0, unroll=8)

        for copy in flying:
            copy.wait_recv()

        def rest(r, carry):
            begin, end = off_ref[0, r], off_ref[0, r + 1]
            xs, ws = [], []
            for k in range(1, MAXR):
                slot = jnp.minimum(begin + k, nnz - 1)
                col = jnp.where(begin + k < end, col_ref[0, slot], none)
                xs.append(ext[col])
                ws.append(w_ref[slot])
            total = acc_ref[r] + dot_nt(jnp.concatenate(xs, axis=1), jnp.concatenate(ws, axis=1))
            cols = pl.ds(pl.multiple_of(r * blk, blk), blk)
            scale = scale_ref[pl.ds(r, 1), :]
            field = ALPHA * scale * total + (1.0 - ALPHA) * seeds_ref[:, cols]
            if step == ITERS - 1:
                out_ref[:, cols] = field
            else:
                scaled = (field * scale).astype(jnp.bfloat16)
                own_ref[r] = scaled
                ext_refs[step + 1][r] = scaled
            return carry

        lax.fori_loop(0, nrb, rest, 0, unroll=8)

    for copy in copies:
        copy.wait_send()


def on_device(blocks, col_index, row_offsets, send_index, deg_scale, seeds):
    nnz, blk = blocks.shape[0], blocks.shape[1]
    width = seeds.shape[0]
    nrb = deg_scale.shape[0] // blk
    parts, per = send_index.shape[1], send_index.shape[2]
    n = lax.axis_size("dom")
    smem = pl.BlockSpec(memory_space=pltpu.SMEM)
    vmem = pl.BlockSpec(memory_space=pltpu.VMEM)
    return pl.pallas_call(
        functools.partial(kernel, n),
        out_shape=jax.ShapeDtypeStruct(seeds.shape, jnp.float32),
        in_specs=[smem, smem, smem, vmem, vmem, pl.BlockSpec(memory_space=pl.ANY)],
        out_specs=vmem,
        scratch_shapes=[
            pltpu.VMEM((nnz, blk, blk), jnp.bfloat16),
            pltpu.VMEM((nrb, width, blk), jnp.bfloat16),
            pltpu.VMEM((nrb, width, blk), jnp.float32),
            [pltpu.VMEM((nrb + parts * per + 1, width, blk), jnp.bfloat16) for _ in range(ITERS)],
            [pltpu.VMEM((parts * per, width, blk), jnp.bfloat16) for _ in range(ITERS)],
            pltpu.SemaphoreType.DMA((CHUNKS,)),
            pltpu.SemaphoreType.DMA((ITERS, parts)),
            pltpu.SemaphoreType.DMA((ITERS, parts)),
        ],
        compiler_params=pltpu.CompilerParams(
            collective_id=0, has_side_effects=True, vmem_limit_bytes=32 * 1024 * 1024),
        cost_estimate=pl.CostEstimate(
            flops=2 * ITERS * nnz * blk * blk * width,
            bytes_accessed=nnz * blk * blk * 2 + 3 * width * nrb * blk * 4,
            transcendentals=0),
        name="spread_all",
    )(col_index, row_offsets, send_index, deg_scale.reshape(nrb, blk), seeds, blocks)


def solution(mesh):
    in_specs = (
        P("dom", None, None),
        P("dom", None),
        P("dom", None),
        P("dom", None, None),
        P("dom"),
        P(None, "dom"),
    )
    out_specs = P(None, "dom")
    return jax.shard_map(
        on_device, mesh=mesh, in_specs=in_specs, out_specs=out_specs, check_vma=False
    )
```

```python
import functools

import jax
import jax.numpy as jnp
from jax import lax
from jax.experimental import pallas as pl
from jax.experimental.pallas import tpu as pltpu
from jax.sharding import PartitionSpec as P

ITERS = 4
MAXR = 4
OFFSETS = (1, -1, 2, -2, 4, -4)
ORDER = (4, 5, 2, 3, 0, 1)
ALPHA = 0.8
CHUNKS = 4


def dot_nt(a, b):
    return lax.dot_general(a, b, (((1,), (1,)), ((), ())), preferred_element_type=jnp.float32)


def kernel(n, col_hbm, off_hbm, lists_hbm, scale_hbm, seeds_hbm, blocks_ref, out_ref,
           col_ref, off_ref, lists_ref, scale_ref, seeds_ref,
           w_ref, own_ref, acc_ref, ext_refs, send_refs, in_sem, w_sem, send_sem, recv_sem):
    nnz, blk = w_ref.shape[0], w_ref.shape[1]
    nrb, width = own_ref.shape[0], own_ref.shape[1]
    parts, per = lists_ref.shape[0], lists_ref.shape[2]
    none = nrb + parts * per
    me = lax.axis_index("dom")
    partners = [lax.rem(me + (o + n), n) for o in OFFSETS]

    barrier = pltpu.get_barrier_semaphore()
    for p in partners:
        pl.semaphore_signal(barrier, inc=1, device_id=(p,), device_id_type=pl.DeviceIdType.MESH)

    small = []
    pairs = ((seeds_hbm, seeds_ref), (scale_hbm, scale_ref), (lists_hbm, lists_ref),
             (off_hbm, off_ref), (col_hbm, col_ref))
    for i, (src, dst) in enumerate(pairs):
        load = pltpu.make_async_copy(src, dst, in_sem.at[i])
        load.start()
        small.append(load)
    span = nnz // CHUNKS
    loads = []
    for c in range(CHUNKS):
        load = pltpu.make_async_copy(
            blocks_ref.at[pl.ds(c * span, span)], w_ref.at[pl.ds(c * span, span)], w_sem.at[c])
        load.start()
        loads.append(load)

    for ext in ext_refs:
        ext[none] = jnp.zeros((width, blk), jnp.bfloat16)
    for load in small:
        load.wait()

    for r in range(nrb):
        cols = pl.ds(r * blk, blk)
        scaled = (seeds_ref[:, cols] * scale_ref[r:r + 1, :]).astype(jnp.bfloat16)
        own_ref[r] = scaled
        ext_refs[0][r] = scaled

    pl.semaphore_wait(barrier, parts)

    copies = []
    for step in range(ITERS):
        ext, send = ext_refs[step], send_refs[step]
        flying = []
        for j in ORDER:
            for h in range(per):
                send[j * per + h] = own_ref[lists_ref[j, 0, h]]
            copy = pltpu.make_async_remote_copy(
                src_ref=send.at[pl.ds(j * per, per)],
                dst_ref=ext.at[pl.ds(nrb + j * per, per)],
                send_sem=send_sem.at[step, j],
                recv_sem=recv_sem.at[step, j],
                device_id=(partners[j],),
                device_id_type=pl.DeviceIdType.MESH,
            )
            copy.start()
            flying.append(copy)
        copies += flying

        if step == 0:
            for load in loads:
                load.wait()

        def first(r, carry):
            acc_ref[r] = dot_nt(ext[r], w_ref[off_ref[0, r]])
            return carry

        lax.fori_loop(0, nrb, first, 0, unroll=8)

        for copy in flying:
            copy.wait_recv()

        def rest(r, carry):
            begin, end = off_ref[0, r], off_ref[0, r + 1]
            xs, ws = [], []
            for k in range(1, MAXR):
                slot = jnp.minimum(begin + k, nnz - 1)
                col = jnp.where(begin + k < end, col_ref[0, slot], none)
                xs.append(ext[col])
                ws.append(w_ref[slot])
            total = acc_ref[r] + dot_nt(jnp.concatenate(xs, axis=1), jnp.concatenate(ws, axis=1))
            cols = pl.ds(pl.multiple_of(r * blk, blk), blk)
            scale = scale_ref[pl.ds(r, 1), :]
            field = ALPHA * scale * total + (1.0 - ALPHA) * seeds_ref[:, cols]
            if step == ITERS - 1:
                out_ref[:, cols] = field
            else:
                scaled = (field * scale).astype(jnp.bfloat16)
                own_ref[r] = scaled
                ext_refs[step + 1][r] = scaled
            return carry

        lax.fori_loop(0, nrb, rest, 0, unroll=8)

    for copy in copies:
        copy.wait_send()


def on_device(blocks, col_index, row_offsets, send_index, deg_scale, seeds):
    nnz, blk = blocks.shape[0], blocks.shape[1]
    width = seeds.shape[0]
    nrb = deg_scale.shape[0] // blk
    parts, per = send_index.shape[1], send_index.shape[2]
    n = lax.axis_size("dom")
    hbm = pl.BlockSpec(memory_space=pltpu.HBM)
    return pl.pallas_call(
        functools.partial(kernel, n),
        out_shape=jax.ShapeDtypeStruct(seeds.shape, jnp.float32),
        in_specs=[hbm] * 6,
        out_specs=pl.BlockSpec(memory_space=pltpu.VMEM),
        scratch_shapes=[
            pltpu.SMEM(col_index.shape, jnp.int32),
            pltpu.SMEM(row_offsets.shape, jnp.int32),
            pltpu.SMEM((parts, 1, per), jnp.int32),
            pltpu.VMEM((nrb, blk), jnp.float32),
            pltpu.VMEM(seeds.shape, jnp.float32),
            pltpu.VMEM((nnz, blk, blk), jnp.bfloat16),
            pltpu.VMEM((nrb, width, blk), jnp.bfloat16),
            pltpu.VMEM((nrb, width, blk), jnp.float32),
            [pltpu.VMEM((nrb + parts * per + 1, width, blk), jnp.bfloat16) for _ in range(ITERS)],
            [pltpu.VMEM((parts * per, width, blk), jnp.bfloat16) for _ in range(ITERS)],
            pltpu.SemaphoreType.DMA((5,)),
            pltpu.SemaphoreType.DMA((CHUNKS,)),
            pltpu.SemaphoreType.DMA((ITERS, parts)),
            pltpu.SemaphoreType.DMA((ITERS, parts)),
        ],
        compiler_params=pltpu.CompilerParams(
            collective_id=0, has_side_effects=True, vmem_limit_bytes=64 * 1024 * 1024),
        cost_estimate=pl.CostEstimate(
            flops=2 * ITERS * nnz * blk * blk * width,
            bytes_accessed=nnz * blk * blk * 2 + 3 * width * nrb * blk * 4,
            transcendentals=0),
        name="spread_all",
    )(col_index, row_offsets, send_index.transpose(1, 0, 2), deg_scale.reshape(nrb, blk), seeds, blocks)


def solution(mesh):
    in_specs = (
        P("dom", None, None),
        P("dom", None),
        P("dom", None),
        P("dom", None, None),
        P("dom"),
        P(None, "dom"),
    )
    out_specs = P(None, "dom")
    return jax.shard_map(
        on_device, mesh=mesh, in_specs=in_specs, out_specs=out_specs, check_vma=False
    )
```

```python
import functools

import jax
import jax.numpy as jnp
from jax import lax
from jax.experimental import pallas as pl
from jax.experimental.pallas import tpu as pltpu
from jax.sharding import PartitionSpec as P

ITERS = 4
MAXR = 4
OFFSETS = (1, -1, 2, -2, 4, -4)
ORDER = (4, 5, 2, 3, 0, 1)
ALPHA = 0.8
CHUNKS = 4


def dot_nt(x, w):
    turned = lax.dot_general(w, x, (((1,), (1,)), ((), ())), preferred_element_type=jnp.float32)
    return turned.T


def kernel(n, col_hbm, off_hbm, lists_hbm, scale_hbm, seeds_hbm, blocks_ref, out_ref,
           col_ref, off_ref, lists_ref, scale_ref, seeds_ref,
           w_ref, own_ref, acc_ref, ext_refs, send_refs, in_sem, w_sem, send_sem, recv_sem):
    nnz, blk = w_ref.shape[0], w_ref.shape[1]
    nrb, width = own_ref.shape[0], own_ref.shape[1]
    parts, per = lists_ref.shape[0], lists_ref.shape[2]
    none = nrb + parts * per
    me = lax.axis_index("dom")
    partners = [lax.rem(me + (o + n), n) for o in OFFSETS]

    barrier = pltpu.get_barrier_semaphore()
    for p in partners:
        pl.semaphore_signal(barrier, inc=1, device_id=(p,), device_id_type=pl.DeviceIdType.MESH)

    small = []
    pairs = ((seeds_hbm, seeds_ref), (scale_hbm, scale_ref), (lists_hbm, lists_ref),
             (off_hbm, off_ref), (col_hbm, col_ref))
    for i, (src, dst) in enumerate(pairs):
        load = pltpu.make_async_copy(src, dst, in_sem.at[i])
        load.start()
        small.append(load)
    span = nnz // CHUNKS
    loads = []
    for c in range(CHUNKS):
        load = pltpu.make_async_copy(
            blocks_ref.at[pl.ds(c * span, span)], w_ref.at[pl.ds(c * span, span)], w_sem.at[c])
        load.start()
        loads.append(load)

    for ext in ext_refs:
        ext[none] = jnp.zeros((width, blk), jnp.bfloat16)
    for load in small:
        load.wait()

    for r in range(nrb):
        cols = pl.ds(r * blk, blk)
        scaled = (seeds_ref[:, cols] * scale_ref[r:r + 1, :]).astype(jnp.bfloat16)
        own_ref[r] = scaled
        ext_refs[0][r] = scaled

    pl.semaphore_wait(barrier, parts)

    copies = []
    for step in range(ITERS):
        ext, send = ext_refs[step], send_refs[step]
        flying = []
        for j in ORDER:
            for h in range(per):
                send[j * per + h] = own_ref[lists_ref[j, 0, h]]
            copy = pltpu.make_async_remote_copy(
                src_ref=send.at[pl.ds(j * per, per)],
                dst_ref=ext.at[pl.ds(nrb + j * per, per)],
                send_sem=send_sem.at[step, j],
                recv_sem=recv_sem.at[step, j],
                device_id=(partners[j],),
                device_id_type=pl.DeviceIdType.MESH,
            )
            copy.start()
            flying.append(copy)
        copies += flying

        if step == 0:
            for load in loads:
                load.wait()

        def first(r, carry):
            acc_ref[r] = dot_nt(ext[r], w_ref[off_ref[0, r]])
            return carry

        lax.fori_loop(0, nrb, first, 0, unroll=True)

        for copy in flying:
            copy.wait_recv()

        def rest(r, carry):
            begin, end = off_ref[0, r], off_ref[0, r + 1]
            xs, ws = [], []
            for k in range(1, MAXR):
                slot = jnp.minimum(begin + k, nnz - 1)
                col = jnp.where(begin + k < end, col_ref[0, slot], none)
                xs.append(ext[col])
                ws.append(w_ref[slot])
            total = acc_ref[r] + dot_nt(jnp.concatenate(xs, axis=1), jnp.concatenate(ws, axis=1))
            cols = pl.ds(pl.multiple_of(r * blk, blk), blk)
            scale = scale_ref[pl.ds(r, 1), :]
            field = ALPHA * scale * total + (1.0 - ALPHA) * seeds_ref[:, cols]
            if step == ITERS - 1:
                out_ref[:, cols] = field
            else:
                scaled = (field * scale).astype(jnp.bfloat16)
                own_ref[r] = scaled
                ext_refs[step + 1][r] = scaled
            return carry

        lax.fori_loop(0, nrb, rest, 0, unroll=True)

    for copy in copies:
        copy.wait_send()


def on_device(blocks, col_index, row_offsets, send_index, deg_scale, seeds):
    nnz, blk = blocks.shape[0], blocks.shape[1]
    width = seeds.shape[0]
    nrb = deg_scale.shape[0] // blk
    parts, per = send_index.shape[1], send_index.shape[2]
    n = lax.axis_size("dom")
    hbm = pl.BlockSpec(memory_space=pltpu.HBM)
    return pl.pallas_call(
        functools.partial(kernel, n),
        out_shape=jax.ShapeDtypeStruct(seeds.shape, jnp.float32),
        in_specs=[hbm] * 6,
        out_specs=pl.BlockSpec(memory_space=pltpu.VMEM),
        scratch_shapes=[
            pltpu.SMEM(col_index.shape, jnp.int32),
            pltpu.SMEM(row_offsets.shape, jnp.int32),
            pltpu.SMEM((parts, 1, per), jnp.int32),
            pltpu.VMEM((nrb, blk), jnp.float32),
            pltpu.VMEM(seeds.shape, jnp.float32),
            pltpu.VMEM((nnz, blk, blk), jnp.bfloat16),
            pltpu.VMEM((nrb, width, blk), jnp.bfloat16),
            pltpu.VMEM((nrb, width, blk), jnp.float32),
            [pltpu.VMEM((nrb + parts * per + 1, width, blk), jnp.bfloat16) for _ in range(ITERS)],
            [pltpu.VMEM((parts * per, width, blk), jnp.bfloat16) for _ in range(ITERS)],
            pltpu.SemaphoreType.DMA((5,)),
            pltpu.SemaphoreType.DMA((CHUNKS,)),
            pltpu.SemaphoreType.DMA((ITERS, parts)),
            pltpu.SemaphoreType.DMA((ITERS, parts)),
        ],
        compiler_params=pltpu.CompilerParams(
            collective_id=0, has_side_effects=True, vmem_limit_bytes=64 * 1024 * 1024),
        cost_estimate=pl.CostEstimate(
            flops=2 * ITERS * nnz * blk * blk * width,
            bytes_accessed=nnz * blk * blk * 2 + 3 * width * nrb * blk * 4,
            transcendentals=0),
        name="spread_all",
    )(col_index, row_offsets, send_index.transpose(1, 0, 2), deg_scale.reshape(nrb, blk), seeds, blocks)


def solution(mesh):
    in_specs = (
        P("dom", None, None),
        P("dom", None),
        P("dom", None),
        P("dom", None, None),
        P("dom"),
        P(None, "dom"),
    )
    out_specs = P(None, "dom")
    return jax.shard_map(
        on_device, mesh=mesh, in_specs=in_specs, out_specs=out_specs, check_vma=False
    )
```

```python
import functools

import jax
import jax.numpy as jnp
from jax import lax
from jax.experimental import pallas as pl
from jax.experimental.pallas import tpu as pltpu
from jax.sharding import PartitionSpec as P

ITERS = 4
MAXR = 4
OFFSETS = (1, -1, 2, -2, 4, -4)
ORDER = (4, 5, 2, 3, 0, 1)
ALPHA = 0.8
CHUNKS = 4
GROUP = 4


def grouped(xs, ws):
    zero = jnp.zeros_like(xs[0])
    count = len(xs)
    placed = [jnp.concatenate([xs[i] if k == i else zero for k in range(count)], axis=1)
              for i in range(count)]
    turned = lax.dot_general(
        jnp.concatenate(ws, axis=1), jnp.concatenate(placed, axis=0),
        (((1,), (1,)), ((), ())), preferred_element_type=jnp.float32)
    return turned.T


def kernel(n, col_hbm, off_hbm, lists_hbm, scale_hbm, seeds_hbm, blocks_ref, out_ref,
           col_ref, off_ref, lists_ref, scale_ref, seeds_ref,
           w_ref, own_ref, acc_ref, ext_refs, send_refs, in_sem, w_sem, send_sem, recv_sem):
    nnz, blk = w_ref.shape[0], w_ref.shape[1]
    nrb, width = own_ref.shape[0], own_ref.shape[1]
    parts, per = lists_ref.shape[0], lists_ref.shape[2]
    none = nrb + parts * per
    me = lax.axis_index("dom")
    partners = [lax.rem(me + (o + n), n) for o in OFFSETS]

    barrier = pltpu.get_barrier_semaphore()
    for p in partners:
        pl.semaphore_signal(barrier, inc=1, device_id=(p,), device_id_type=pl.DeviceIdType.MESH)

    small = []
    pairs = ((seeds_hbm, seeds_ref), (scale_hbm, scale_ref), (lists_hbm, lists_ref),
             (off_hbm, off_ref), (col_hbm, col_ref))
    for i, (src, dst) in enumerate(pairs):
        load = pltpu.make_async_copy(src, dst, in_sem.at[i])
        load.start()
        small.append(load)
    span = nnz // CHUNKS
    loads = []
    for c in range(CHUNKS):
        load = pltpu.make_async_copy(
            blocks_ref.at[pl.ds(c * span, span)], w_ref.at[pl.ds(c * span, span)], w_sem.at[c])
        load.start()
        loads.append(load)

    for ext in ext_refs:
        ext[none] = jnp.zeros((width, blk), jnp.bfloat16)
    for load in small:
        load.wait()

    for r in range(nrb):
        cols = pl.ds(r * blk, blk)
        scaled = (seeds_ref[:, cols] * scale_ref[r:r + 1, :]).astype(jnp.bfloat16)
        own_ref[r] = scaled
        ext_refs[0][r] = scaled

    pl.semaphore_wait(barrier, parts)

    copies = []
    for step in range(ITERS):
        ext, send = ext_refs[step], send_refs[step]
        flying = []
        for j in ORDER:
            for h in range(per):
                send[j * per + h] = own_ref[lists_ref[j, 0, h]]
            copy = pltpu.make_async_remote_copy(
                src_ref=send.at[pl.ds(j * per, per)],
                dst_ref=ext.at[pl.ds(nrb + j * per, per)],
                send_sem=send_sem.at[step, j],
                recv_sem=recv_sem.at[step, j],
                device_id=(partners[j],),
                device_id_type=pl.DeviceIdType.MESH,
            )
            copy.start()
            flying.append(copy)
        copies += flying

        if step == 0:
            for load in loads:
                load.wait()

        def first(g, carry):
            rows = [g * GROUP + i for i in range(GROUP)]
            acc_ref[g] = grouped([ext[r] for r in rows], [w_ref[off_ref[0, r]] for r in rows])
            return carry

        lax.fori_loop(0, nrb // GROUP, first, 0, unroll=True)

        for copy in flying:
            copy.wait_recv()

        def rest(g, carry):
            rows = [g * GROUP + i for i in range(GROUP)]
            xs, ws = [], []
            for r in rows:
                begin, end = off_ref[0, r], off_ref[0, r + 1]
                x, w = [], []
                for k in range(1, MAXR):
                    slot = jnp.minimum(begin + k, nnz - 1)
                    col = jnp.where(begin + k < end, col_ref[0, slot], none)
                    x.append(ext[col])
                    w.append(w_ref[slot])
                xs.append(jnp.concatenate(x, axis=1))
                ws.append(jnp.concatenate(w, axis=1))
            totals = acc_ref[g] + grouped(xs, ws)
            for i, r in enumerate(rows):
                total = totals[i * width:(i + 1) * width]
                cols = pl.ds(pl.multiple_of(r * blk, blk), blk)
                scale = scale_ref[pl.ds(r, 1), :]
                field = ALPHA * scale * total + (1.0 - ALPHA) * seeds_ref[:, cols]
                if step == ITERS - 1:
                    out_ref[:, cols] = field
                else:
                    scaled = (field * scale).astype(jnp.bfloat16)
                    own_ref[r] = scaled
                    ext_refs[step + 1][r] = scaled
            return carry

        lax.fori_loop(0, nrb // GROUP, rest, 0, unroll=True)

    for copy in copies:
        copy.wait_send()


def on_device(blocks, col_index, row_offsets, send_index, deg_scale, seeds):
    nnz, blk = blocks.shape[0], blocks.shape[1]
    width = seeds.shape[0]
    nrb = deg_scale.shape[0] // blk
    parts, per = send_index.shape[1], send_index.shape[2]
    n = lax.axis_size("dom")
    hbm = pl.BlockSpec(memory_space=pltpu.HBM)
    return pl.pallas_call(
        functools.partial(kernel, n),
        out_shape=jax.ShapeDtypeStruct(seeds.shape, jnp.float32),
        in_specs=[hbm] * 6,
        out_specs=pl.BlockSpec(memory_space=pltpu.VMEM),
        scratch_shapes=[
            pltpu.SMEM(col_index.shape, jnp.int32),
            pltpu.SMEM(row_offsets.shape, jnp.int32),
            pltpu.SMEM((parts, 1, per), jnp.int32),
            pltpu.VMEM((nrb, blk), jnp.float32),
            pltpu.VMEM(seeds.shape, jnp.float32),
            pltpu.VMEM((nnz, blk, blk), jnp.bfloat16),
            pltpu.VMEM((nrb, width, blk), jnp.bfloat16),
            pltpu.VMEM((nrb // GROUP, GROUP * width, blk), jnp.float32),
            [pltpu.VMEM((nrb + parts * per + 1, width, blk), jnp.bfloat16) for _ in range(ITERS)],
            [pltpu.VMEM((parts * per, width, blk), jnp.bfloat16) for _ in range(ITERS)],
            pltpu.SemaphoreType.DMA((5,)),
            pltpu.SemaphoreType.DMA((CHUNKS,)),
            pltpu.SemaphoreType.DMA((ITERS, parts)),
            pltpu.SemaphoreType.DMA((ITERS, parts)),
        ],
        compiler_params=pltpu.CompilerParams(
            collective_id=0, has_side_effects=True, vmem_limit_bytes=64 * 1024 * 1024),
        cost_estimate=pl.CostEstimate(
            flops=2 * ITERS * nnz * blk * blk * width,
            bytes_accessed=nnz * blk * blk * 2 + 3 * width * nrb * blk * 4,
            transcendentals=0),
        name="spread_all",
    )(col_index, row_offsets, send_index.transpose(1, 0, 2), deg_scale.reshape(nrb, blk), seeds, blocks)


def solution(mesh):
    in_specs = (
        P("dom", None, None),
        P("dom", None),
        P("dom", None),
        P("dom", None, None),
        P("dom"),
        P(None, "dom"),
    )
    out_specs = P(None, "dom")
    return jax.shard_map(
        on_device, mesh=mesh, in_specs=in_specs, out_specs=out_specs, check_vma=False
    )
```

```python
import functools

import jax
import jax.numpy as jnp
from jax import lax
from jax.experimental import pallas as pl
from jax.experimental.pallas import tpu as pltpu
from jax.sharding import PartitionSpec as P

ITERS = 4
MAXR = 4
OFFSETS = (1, -1, 2, -2, 4, -4)
ORDER = (4, 5, 2, 3, 0, 1)
ALPHA = 0.8
CHUNKS = 4


def dot_nt(x, w):
    turned = lax.dot_general(w, x, (((1,), (1,)), ((), ())), preferred_element_type=jnp.float32)
    return turned.T


def kernel(n, col_hbm, off_hbm, lists_hbm, scale_hbm, seeds_hbm, blocks_ref, out_ref,
           col_ref, off_ref, lists_ref, scale_ref, seeds_ref,
           w_ref, own_ref, acc_ref, ext_refs, send_refs, in_sem, w_sem, send_sem, recv_sem):
    nnz, blk = w_ref.shape[0], w_ref.shape[1]
    nrb, width = own_ref.shape[0], own_ref.shape[1]
    parts, per = lists_ref.shape[0], lists_ref.shape[2]
    none = nrb + parts * per
    me = lax.axis_index("dom")
    partners = [lax.rem(me + (o + n), n) for o in OFFSETS]

    barrier = pltpu.get_barrier_semaphore()
    for p in partners:
        pl.semaphore_signal(barrier, inc=1, device_id=(p,), device_id_type=pl.DeviceIdType.MESH)

    small = []
    pairs = ((seeds_hbm, seeds_ref), (scale_hbm, scale_ref), (lists_hbm, lists_ref),
             (off_hbm, off_ref), (col_hbm, col_ref))
    for i, (src, dst) in enumerate(pairs):
        load = pltpu.make_async_copy(src, dst, in_sem.at[i])
        load.start()
        small.append(load)
    span = nnz // CHUNKS
    loads = []
    for c in range(CHUNKS):
        load = pltpu.make_async_copy(
            blocks_ref.at[pl.ds(c * span, span)], w_ref.at[pl.ds(c * span, span)], w_sem.at[c])
        load.start()
        loads.append(load)

    for ext in ext_refs:
        ext[none] = jnp.zeros((width, blk), jnp.bfloat16)
    for load in small:
        load.wait()

    for r in range(nrb):
        cols = pl.ds(r * blk, blk)
        scaled = (seeds_ref[:, cols] * scale_ref[r:r + 1, :]).astype(jnp.bfloat16)
        own_ref[r] = scaled
        ext_refs[0][r] = scaled

    pl.semaphore_wait(barrier, parts)

    copies = []
    for step in range(ITERS):
        ext, send = ext_refs[step], send_refs[step]
        flying = []
        for j in ORDER:
            for h in range(per):
                send[j * per + h] = own_ref[lists_ref[j, 0, h]]
            copy = pltpu.make_async_remote_copy(
                src_ref=send.at[pl.ds(j * per, per)],
                dst_ref=ext.at[pl.ds(nrb + j * per, per)],
                send_sem=send_sem.at[step, j],
                recv_sem=recv_sem.at[step, j],
                device_id=(partners[j],),
                device_id_type=pl.DeviceIdType.MESH,
            )
            copy.start()
            flying.append(copy)
        copies += flying

        if step == 0:
            for load in loads:
                load.wait()

        def first(r, carry):
            acc_ref[r] = dot_nt(ext[r], w_ref[off_ref[0, r]])
            return carry

        lax.fori_loop(0, nrb, first, 0, unroll=True)

        for copy in flying:
            copy.wait_recv()

        def rest(r, carry):
            begin, end = off_ref[0, r], off_ref[0, r + 1]
            xs, ws = [], []
            for k in range(1, MAXR):
                slot = jnp.minimum(begin + k, nnz - 1)
                col = jnp.where(begin + k < end, col_ref[0, slot], none)
                xs.append(ext[col])
                ws.append(w_ref[slot])
            total = acc_ref[r] + dot_nt(jnp.concatenate(xs, axis=1), jnp.concatenate(ws, axis=1))
            cols = pl.ds(pl.multiple_of(r * blk, blk), blk)
            scale = scale_ref[pl.ds(r, 1), :]
            field = ALPHA * scale * total + (1.0 - ALPHA) * seeds_ref[:, cols]
            if step == ITERS - 1:
                out_ref[:, cols] = total
            else:
                scaled = (field * scale).astype(jnp.bfloat16)
                own_ref[r] = scaled
                ext_refs[step + 1][r] = scaled
            return carry

        lax.fori_loop(0, nrb, rest, 0, unroll=True)

    for copy in copies:
        copy.wait_send()


def on_device(blocks, col_index, row_offsets, send_index, deg_scale, seeds):
    nnz, blk = blocks.shape[0], blocks.shape[1]
    width = seeds.shape[0]
    nrb = deg_scale.shape[0] // blk
    parts, per = send_index.shape[1], send_index.shape[2]
    n = lax.axis_size("dom")
    hbm = pl.BlockSpec(memory_space=pltpu.HBM)
    product = pl.pallas_call(
        functools.partial(kernel, n),
        out_shape=jax.ShapeDtypeStruct(seeds.shape, jnp.float32),
        in_specs=[hbm] * 6,
        out_specs=pl.BlockSpec(memory_space=pltpu.VMEM),
        scratch_shapes=[
            pltpu.SMEM(col_index.shape, jnp.int32),
            pltpu.SMEM(row_offsets.shape, jnp.int32),
            pltpu.SMEM((parts, 1, per), jnp.int32),
            pltpu.VMEM((nrb, blk), jnp.float32),
            pltpu.VMEM(seeds.shape, jnp.float32),
            pltpu.VMEM((nnz, blk, blk), jnp.bfloat16),
            pltpu.VMEM((nrb, width, blk), jnp.bfloat16),
            pltpu.VMEM((nrb, width, blk), jnp.float32),
            [pltpu.VMEM((nrb + parts * per + 1, width, blk), jnp.bfloat16) for _ in range(ITERS)],
            [pltpu.VMEM((parts * per, width, blk), jnp.bfloat16) for _ in range(ITERS)],
            pltpu.SemaphoreType.DMA((5,)),
            pltpu.SemaphoreType.DMA((CHUNKS,)),
            pltpu.SemaphoreType.DMA((ITERS, parts)),
            pltpu.SemaphoreType.DMA((ITERS, parts)),
        ],
        compiler_params=pltpu.CompilerParams(
            collective_id=0, has_side_effects=True, vmem_limit_bytes=64 * 1024 * 1024),
        cost_estimate=pl.CostEstimate(
            flops=2 * ITERS * nnz * blk * blk * width,
            bytes_accessed=nnz * blk * blk * 2 + 3 * width * nrb * blk * 4,
            transcendentals=0),
        name="spread_all",
    )(col_index, row_offsets, send_index.transpose(1, 0, 2), deg_scale.reshape(nrb, blk), seeds, blocks)
    return ALPHA * deg_scale[None, :] * product + (1.0 - ALPHA) * seeds


def solution(mesh):
    in_specs = (
        P("dom", None, None),
        P("dom", None),
        P("dom", None),
        P("dom", None, None),
        P("dom"),
        P(None, "dom"),
    )
    out_specs = P(None, "dom")
    return jax.shard_map(
        on_device, mesh=mesh, in_specs=in_specs, out_specs=out_specs, check_vma=False
    )
```

```python
import functools

import jax
import jax.numpy as jnp
from jax import lax
from jax.experimental import pallas as pl
from jax.experimental.pallas import tpu as pltpu
from jax.sharding import PartitionSpec as P

ITERS = 4
MAXR = 4
OFFSETS = (1, -1, 2, -2, 4, -4)
ORDER = (4, 5, 2, 3, 0, 1)
ALPHA = 0.8
CHUNKS = 4


def dot_nt(x, w):
    turned = lax.dot_general(w, x, (((1,), (1,)), ((), ())), preferred_element_type=jnp.float32)
    return turned.T


def kernel(n, col_hbm, off_hbm, lists_hbm, scale_hbm, seeds_hbm, blocks_ref, out_hbm,
           col_ref, off_ref, lists_ref, scale_ref, seeds_ref,
           out_ref, w_ref, own_ref, acc_ref, ext_refs, send_refs, out_sem, in_sem, w_sem, send_sem, recv_sem):
    nnz, blk = w_ref.shape[0], w_ref.shape[1]
    nrb, width = own_ref.shape[0], own_ref.shape[1]
    parts, per = lists_ref.shape[0], lists_ref.shape[2]
    none = nrb + parts * per
    me = lax.axis_index("dom")
    partners = [lax.rem(me + (o + n), n) for o in OFFSETS]

    barrier = pltpu.get_barrier_semaphore()
    for p in partners:
        pl.semaphore_signal(barrier, inc=1, device_id=(p,), device_id_type=pl.DeviceIdType.MESH)

    small = []
    pairs = ((seeds_hbm, seeds_ref), (scale_hbm, scale_ref), (lists_hbm, lists_ref),
             (off_hbm, off_ref), (col_hbm, col_ref))
    for i, (src, dst) in enumerate(pairs):
        load = pltpu.make_async_copy(src, dst, in_sem.at[i])
        load.start()
        small.append(load)
    span = nnz // CHUNKS
    loads = []
    for c in range(CHUNKS):
        load = pltpu.make_async_copy(
            blocks_ref.at[pl.ds(c * span, span)], w_ref.at[pl.ds(c * span, span)], w_sem.at[c])
        load.start()
        loads.append(load)

    for ext in ext_refs:
        ext[none] = jnp.zeros((width, blk), jnp.bfloat16)
    for load in small:
        load.wait()

    for r in range(nrb):
        cols = pl.ds(r * blk, blk)
        scaled = (seeds_ref[:, cols] * scale_ref[r:r + 1, :]).astype(jnp.bfloat16)
        own_ref[r] = scaled
        ext_refs[0][r] = scaled

    pl.semaphore_wait(barrier, parts)

    copies = []
    for step in range(ITERS):
        ext, send = ext_refs[step], send_refs[step]
        flying = []
        for j in ORDER:
            for h in range(per):
                send[j * per + h] = own_ref[lists_ref[j, 0, h]]
            copy = pltpu.make_async_remote_copy(
                src_ref=send.at[pl.ds(j * per, per)],
                dst_ref=ext.at[pl.ds(nrb + j * per, per)],
                send_sem=send_sem.at[step, j],
                recv_sem=recv_sem.at[step, j],
                device_id=(partners[j],),
                device_id_type=pl.DeviceIdType.MESH,
            )
            copy.start()
            flying.append(copy)
        copies += flying

        if step == 0:
            for load in loads:
                load.wait()

        def first(r, carry):
            acc_ref[r] = dot_nt(ext[r], w_ref[off_ref[0, r]])
            return carry

        lax.fori_loop(0, nrb, first, 0, unroll=True)

        for copy in flying:
            copy.wait_recv()

        def rest(r, carry):
            begin, end = off_ref[0, r], off_ref[0, r + 1]
            xs, ws = [], []
            for k in range(1, MAXR):
                slot = jnp.minimum(begin + k, nnz - 1)
                col = jnp.where(begin + k < end, col_ref[0, slot], none)
                xs.append(ext[col])
                ws.append(w_ref[slot])
            total = acc_ref[r] + dot_nt(jnp.concatenate(xs, axis=1), jnp.concatenate(ws, axis=1))
            cols = pl.ds(pl.multiple_of(r * blk, blk), blk)
            scale = scale_ref[pl.ds(r, 1), :]
            field = ALPHA * scale * total + (1.0 - ALPHA) * seeds_ref[:, cols]
            if step == ITERS - 1:
                out_ref[:, cols] = field
            else:
                scaled = (field * scale).astype(jnp.bfloat16)
                own_ref[r] = scaled
                ext_refs[step + 1][r] = scaled
            return carry

        if step < ITERS - 1:
            lax.fori_loop(0, nrb, rest, 0, unroll=True)

    results = []
    part = nrb // CHUNKS
    for c in range(CHUNKS):
        lax.fori_loop(c * part, (c + 1) * part, rest, 0, unroll=True)
        cols = pl.ds(c * part * blk, part * blk)
        result = pltpu.make_async_copy(out_ref.at[:, cols], out_hbm.at[:, cols], out_sem.at[c])
        result.start()
        results.append(result)
    for result in results:
        result.wait()

    for copy in copies:
        copy.wait_send()


def on_device(blocks, col_index, row_offsets, send_index, deg_scale, seeds):
    nnz, blk = blocks.shape[0], blocks.shape[1]
    width = seeds.shape[0]
    nrb = deg_scale.shape[0] // blk
    parts, per = send_index.shape[1], send_index.shape[2]
    n = lax.axis_size("dom")
    hbm = pl.BlockSpec(memory_space=pltpu.HBM)
    return pl.pallas_call(
        functools.partial(kernel, n),
        out_shape=jax.ShapeDtypeStruct(seeds.shape, jnp.float32),
        in_specs=[hbm] * 6,
        out_specs=hbm,
        scratch_shapes=[
            pltpu.SMEM(col_index.shape, jnp.int32),
            pltpu.SMEM(row_offsets.shape, jnp.int32),
            pltpu.SMEM((parts, 1, per), jnp.int32),
            pltpu.VMEM((nrb, blk), jnp.float32),
            pltpu.VMEM(seeds.shape, jnp.float32),
            pltpu.VMEM(seeds.shape, jnp.float32),
            pltpu.VMEM((nnz, blk, blk), jnp.bfloat16),
            pltpu.VMEM((nrb, width, blk), jnp.bfloat16),
            pltpu.VMEM((nrb, width, blk), jnp.float32),
            [pltpu.VMEM((nrb + parts * per + 1, width, blk), jnp.bfloat16) for _ in range(ITERS)],
            [pltpu.VMEM((parts * per, width, blk), jnp.bfloat16) for _ in range(ITERS)],
            pltpu.SemaphoreType.DMA((CHUNKS,)),
            pltpu.SemaphoreType.DMA((5,)),
            pltpu.SemaphoreType.DMA((CHUNKS,)),
            pltpu.SemaphoreType.DMA((ITERS, parts)),
            pltpu.SemaphoreType.DMA((ITERS, parts)),
        ],
        compiler_params=pltpu.CompilerParams(
            collective_id=0, has_side_effects=True, vmem_limit_bytes=64 * 1024 * 1024),
        cost_estimate=pl.CostEstimate(
            flops=2 * ITERS * nnz * blk * blk * width,
            bytes_accessed=nnz * blk * blk * 2 + 3 * width * nrb * blk * 4,
            transcendentals=0),
        name="spread_all",
    )(col_index, row_offsets, send_index.transpose(1, 0, 2), deg_scale.reshape(nrb, blk), seeds, blocks)


def solution(mesh):
    in_specs = (
        P("dom", None, None),
        P("dom", None),
        P("dom", None),
        P("dom", None, None),
        P("dom"),
        P(None, "dom"),
    )
    out_specs = P(None, "dom")
    return jax.shard_map(
        on_device, mesh=mesh, in_specs=in_specs, out_specs=out_specs, check_vma=False
    )
```
